32 devices in a mesh: groups: 2 (over x), wide: 16 (over z, y, core).
Axes of the slice: x: 2, y: 2, z: 4, core: 2. Of those that a mesh axis runs over, the one named last changes fastest.
Arguments:
- tokens: bfloat16 [128, 16384], P('groups', 'wide'), parts along dimension 0, may hold values from -1.5 to 1.5
- norm_gain: bfloat16 [16384], P('wide'), may hold values from 0.099609375 to 1.8984375
- w_query: bfloat16 [16384, 8192], P('wide'), may hold values from -0.046875 to 0.046875
- key_weight: bfloat16 [16384, 512], P('wide'), may hold values from -0.046875 to 0.046875
- value_weight: bfloat16 [16384, 512], P('wide'), may hold values from -0.046875 to 0.046875
- w_out: bfloat16 [8192, 16384], P(None, 'wide'), may hold values from -0.0625 to 0.0625
- cache_keys: bfloat16 [128, 1024, 512], P(('groups', 'wide')), parts along dimension 0, may hold values from -1210 to 1210
- value_cache_slots: bfloat16 [128, 1024, 512], P(('groups', 'wide')), parts along dimension 0, may hold values from -6 to 6
- slot_fill_lengths: int32 [128], P(('groups', 'wide')), parts along dimension 0, may hold values from 1 to 1023, as said below
- slot_rows: int32 [128], P('groups'), parts along dimension 0, may hold values from 0 to 63, each once
Outputs:
- mixed: bfloat16 [128, 16384], P('groups', 'wide'), parts along dimension 0
- new_entries: bfloat16 [2, 128, 512], P(None, ('groups', 'wide')), parts along dimension 1
The draws below stay inside these ranges and needn't reach their ends.
There are 2 independent parts, one for each index of `groups`. The reference program is written for one: setup_inputs(seed, part) draws one part's arguments, and reference() takes and returns one part's arrays. A program takes and returns all parts, laid end to end along the dimension named above; an argument that names none is the same for every part. Nothing has to cross between parts.
Inputs may be any that keep to these rules, and one draw needn't show every extreme that they name: `slot_fill_lengths`: every slot has at least one filled position and room for the new token; some slot is filled to 1023 and some to 1.
All inputs are finite; a program needn't handle non-finite values.
Results may differ from the reference program's by a relative error of at most 0.012.
The reference program's roundings to bfloat16 on the way (of `ordered`, `gained`, `rounded` and `heads`) count: a program that leaves them out, or rounds other values in their place, can miss the bound.
Values may be sent and summed in bfloat16 or wider, within the bound.
A program may use at most 128 MiB of HBM per device.

```python
import jax
import jax.numpy as jnp
from jax import lax

MODEL_WIDTH = 16384
HEAD_SIZE = 128
QUERY_HEADS = 64
KEY_VALUE_HEADS = 4
SLOT_CAPACITY = 1024
DECODE_ROWS = 64


def slot_lengths(key):
    inner = jax.random.fold_in(key, 11)
    first_key, second_key, third_key = jax.random.split(inner, 3)
    lengths = jax.random.randint(first_key, (DECODE_ROWS,), 1, SLOT_CAPACITY)
    longest = jax.random.randint(second_key, (), 0, DECODE_ROWS)
    shortest = (longest + 1 + jax.random.randint(third_key, (), 0, DECODE_ROWS - 1)) % DECODE_ROWS
    positions = jnp.arange(DECODE_ROWS)
    lengths = jnp.where(positions == shortest, 1, lengths)
    lengths = jnp.where(positions == longest, SLOT_CAPACITY - 1, lengths)
    return lengths.astype(jnp.int32)


def draw_slot_fill_lengths(key, part):
    return slot_lengths(key)


def draw_cache_keys(key, part):
    key = jax.random.fold_in(key, 5)
    random_root_key = jax.random.fold_in(key, 0)
    slot_keys = jnp.clip(jax.random.normal(random_root_key, (DECODE_ROWS, SLOT_CAPACITY, KEY_VALUE_HEADS * HEAD_SIZE)), -6.0, 6.0)
    return slot_keys.astype(jnp.bfloat16)


def levels(own_key, shape, cuts, smallest, top_value):
    def one(position, shards_of):
        steps = jax.random.uniform(jax.random.fold_in(jax.random.fold_in(own_key, 6), position), (shards_of,), jnp.float32, smallest / len(cuts), top_value / len(cuts))
        return jnp.repeat(jnp.exp(steps), shape[position] // shards_of).reshape((-1,) + (1,) * (len(shape) - position - 1))

    factor_of = one(*cuts[0])
    for cut in cuts[1:]:
        factor_of = factor_of * one(*cut)
    return factor_of


def bell_draw(own_key, shape, spread, most, cuts=(), kind=jnp.bfloat16):
    drawn = spread * jax.random.normal(own_key, shape, jnp.float32)
    if cuts:
        drawn = drawn * levels(own_key, shape, cuts, -0.22, 0.18)
    return jnp.clip(drawn, -most, most).astype(kind)


def setup_inputs(seed: int = 0, part: int = 0) -> dict:
    streams_of = jax.random.split(jax.random.key(seed), 11)
    part_keys = jax.random.split(jax.random.fold_in(streams_of[10], part), 11)
    tokens = bell_draw(part_keys[0], (DECODE_ROWS, MODEL_WIDTH), 0.25, 1.5, ((1, 16),))
    norm_gain = jnp.clip(1.0 + 0.18 * jax.random.normal(streams_of[1], (MODEL_WIDTH,), jnp.float32), 0.099609375, 1.8984375).astype(jnp.bfloat16)
    w_query = bell_draw(streams_of[2], (MODEL_WIDTH, QUERY_HEADS * HEAD_SIZE), MODEL_WIDTH ** -0.5, 0.046875, ((0, 16),))
    key_weight = bell_draw(streams_of[3], (MODEL_WIDTH, KEY_VALUE_HEADS * HEAD_SIZE), MODEL_WIDTH ** -0.5, 0.046875, ((0, 16),))
    value_weight = bell_draw(streams_of[4], (MODEL_WIDTH, KEY_VALUE_HEADS * HEAD_SIZE), MODEL_WIDTH ** -0.5, 0.046875, ((0, 16),))
    w_out = bell_draw(streams_of[5], (QUERY_HEADS * HEAD_SIZE, MODEL_WIDTH), (QUERY_HEADS * HEAD_SIZE) ** -0.5, 0.0625, ((1, 16),))
    cache_keys = draw_cache_keys(jax.random.fold_in(jax.random.fold_in(streams_of[10], part), 71), part)
    value_cache_slots = bell_draw(part_keys[7], (DECODE_ROWS, SLOT_CAPACITY, KEY_VALUE_HEADS * HEAD_SIZE), 1.0, 6.0, ((0, 16),))
    slot_fill_lengths = draw_slot_fill_lengths(jax.random.fold_in(jax.random.fold_in(streams_of[10], part), 71), part)
    slot_rows = jax.random.permutation(part_keys[9], DECODE_ROWS).astype(jnp.int32)
    return dict(tokens=tokens, norm_gain=norm_gain, w_query=w_query, key_weight=key_weight, value_weight=value_weight, w_out=w_out, cache_keys=cache_keys, value_cache_slots=value_cache_slots, slot_fill_lengths=slot_fill_lengths, slot_rows=slot_rows)


def apply_rotary(slot_values, positions, heads):
    filled_count = slot_values.shape[0]
    half = HEAD_SIZE // 2
    freq = 500000.0 ** (-(2.0 / HEAD_SIZE) * jnp.arange(half, dtype=jnp.float32))
    angle = positions.astype(jnp.float32)[:, None] * freq[None, :]
    cosine = jnp.cos(angle)[:, None, :]
    sine = jnp.sin(angle)[:, None, :]
    shaped = slot_values.reshape(filled_count, heads, HEAD_SIZE)
    first = shaped[..., :half]
    second = shaped[..., half:]
    joined = jnp.concatenate([first * cosine - second * sine, second * cosine + first * sine], axis=2)
    return joined.reshape(filled_count, heads * HEAD_SIZE)

def attend_slot(operands):
    query_vector, fresh_key, fresh_value, slot_keys, slot_values, length = operands
    query_group = QUERY_HEADS // KEY_VALUE_HEADS
    slot_room = slot_keys.shape[0]
    query_wide_float = query_vector.reshape(KEY_VALUE_HEADS, query_group, HEAD_SIZE).astype(jnp.float32)
    keys_wide_float = slot_keys.reshape(slot_room, KEY_VALUE_HEADS, HEAD_SIZE).astype(jnp.float32)
    values_wide_float = slot_values.reshape(slot_room, KEY_VALUE_HEADS, HEAD_SIZE).astype(jnp.float32)
    scale_factor = HEAD_SIZE ** (-0.5)
    scores = jnp.einsum('kgd,pkd->kgp', query_wide_float, keys_wide_float) * scale_factor
    live = jnp.arange(slot_room, dtype=jnp.int32) < length
    scores = jnp.where(live[None, None, :], scores, -1e+30)
    local_share = jnp.einsum('iox,ix->io', query_wide_float, fresh_key.reshape(KEY_VALUE_HEADS, HEAD_SIZE).astype(jnp.float32)) * scale_factor
    top = jnp.maximum(lax.optimization_barrier(jnp.max(scores, axis=2)), local_share)
    weights = jnp.exp(scores - top[..., None])
    own_weight = jnp.exp(local_share - top)
    total = lax.optimization_barrier(jnp.sum(weights, axis=2)) + own_weight
    rounded = lax.optimization_barrier(weights.astype(jnp.bfloat16)).astype(jnp.float32)
    local_share_rounded = lax.optimization_barrier(own_weight.astype(jnp.bfloat16)).astype(jnp.float32)
    reduced_sum = jnp.einsum('kgp,pkd->kgd', rounded, values_wide_float)
    reduced_sum = reduced_sum + local_share_rounded[..., None] * fresh_value.reshape(KEY_VALUE_HEADS, 1, HEAD_SIZE).astype(jnp.float32)
    return (reduced_sum / total[..., None]).reshape(QUERY_HEADS * HEAD_SIZE).astype(jnp.bfloat16)

def reference(tokens, norm_gain, w_query, key_weight, value_weight, w_out, cache_keys, value_cache_slots, slot_fill_lengths, slot_rows):
    ordered = tokens[slot_rows]
    ordered_f = ordered.astype(jnp.float32)
    squares = lax.optimization_barrier(jnp.sum(ordered_f * ordered_f, axis=1))
    score_scale = lax.rsqrt(squares / MODEL_WIDTH + 1e-05)[:, None]
    gained = (ordered_f * norm_gain.astype(jnp.float32)[None, :]).astype(jnp.bfloat16)
    raw_q = jnp.dot(gained, w_query, preferred_element_type=jnp.float32) * score_scale
    unrotated_key = jnp.dot(gained, key_weight, preferred_element_type=jnp.float32) * score_scale
    projected_value = jnp.dot(gained, value_weight, preferred_element_type=jnp.float32) * score_scale
    query_vector = apply_rotary(raw_q, slot_fill_lengths, QUERY_HEADS).astype(jnp.bfloat16)
    fresh_key = apply_rotary(unrotated_key, slot_fill_lengths, KEY_VALUE_HEADS).astype(jnp.bfloat16)
    fresh_value = projected_value.astype(jnp.bfloat16)
    heads = lax.map(attend_slot, (query_vector, fresh_key, fresh_value, cache_keys, value_cache_slots, slot_fill_lengths))
    projected = jnp.dot(heads, w_out, preferred_element_type=jnp.float32)
    filled_count = slot_rows.shape[0]
    inverse = jnp.zeros((filled_count,), jnp.int32).at[slot_rows].set(jnp.arange(filled_count, dtype=jnp.int32))
    mixed = (tokens.astype(jnp.float32) + projected[inverse]).astype(jnp.bfloat16)
    return (mixed, jnp.stack([fresh_key, fresh_value]))
```

```python
import functools

import jax
import jax.numpy as jnp
import numpy as np
from jax import lax
from jax.experimental import pallas as pl
from jax.experimental.pallas import tpu as pltpu
from jax.sharding import PartitionSpec as P

HEAD = 128
KV_HEADS = 4
GROUP = 16
QCOLS = GROUP * HEAD
KVCOLS = KV_HEADS * HEAD
SIDE = 2 * KVCOLS + HEAD
F32 = jnp.float32
BF16 = jnp.bfloat16
NT = (((1,), (1,)), ((), ()))


def iota(shape, axis):
    return lax.broadcasted_iota(jnp.int32, shape, axis)


def one_hot(condition):
    return jnp.where(condition, 1.0, 0.0).astype(BF16)


def reversed_bits(value, bits):
    out = jnp.zeros_like(value)
    for b in range(bits):
        out = out + ((value >> b) & 1) * (1 << (bits - 1 - b))
    return out


def dot(a, b):
    return jnp.dot(a, b, preferred_element_type=F32)


def kernel(n, stages, local, room, width,
           lengths, tokens, gain, rows_of, freq, wq_hbm, wk_hbm, wv_hbm, wo_hbm, kc_hbm, vc_hbm,
           mixed, entries,
           wq, wk, wv, wo, kc, vc, gained, side, queries, *rest):
    side_in = rest[:stages]
    query_in = rest[stages:2 * stages]
    (side_out, query_out, gathered, qs, hs, cos_tile, sin_tile, fresh, picks, total_out,
     w_sem, rs_send, rs_recv, ag_send, ag_recv) = rest[2 * stages:]
    rows = n * local
    parts = 16 // local
    per = GROUP // parts
    block = 16
    me = lax.axis_index("wide")
    bits = [(me // (1 << b)) % 2 for b in range(stages)]
    partner = [me + (1 - 2 * bits[b]) * (1 << b) for b in range(stages)]
    base = [jnp.int32(0)]
    for b in range(stages):
        base.append(base[-1] + bits[b] * (n >> (b + 1)))

    def weight_copy(i):
        if i == 0:
            return [pltpu.make_async_copy(wk_hbm, wk, w_sem.at[0]),
                    pltpu.make_async_copy(wv_hbm, wv, w_sem.at[1])]
        if i <= KV_HEADS:
            g = i - 1
            return [pltpu.make_async_copy(wq_hbm.at[:, pl.ds(g * QCOLS, QCOLS)], wq.at[g], w_sem.at[2 + g])]
        if i == KV_HEADS + 1:
            return [pltpu.make_async_copy(kc_hbm, kc, w_sem.at[6]),
                    pltpu.make_async_copy(vc_hbm, vc, w_sem.at[7])]
        g = i - KV_HEADS - 2
        return [pltpu.make_async_copy(wo_hbm.at[pl.ds(g * QCOLS, QCOLS)], wo.at[pl.ds(g * QCOLS, QCOLS)],
                                      w_sem.at[8 + g])]

    def begin(i):
        for c in weight_copy(i):
            c.start()

    def arrived(i):
        for c in weight_copy(i):
            c.wait()

    for i in range(KV_HEADS + 1):
        begin(i)

    barrier = pltpu.get_barrier_semaphore()
    for b in range(stages):
        pl.semaphore_signal(barrier, inc=1, device_id={"wide": partner[b]},
                            device_id_type=pl.DeviceIdType.MESH)

    slot_rows = rows_of[...]
    place = iota((rows, rows), 0)
    slot_at = reversed_bits(place // local, stages) * local + place % local
    reorder = one_hot(slot_at == iota((rows, rows), 1))
    row_of_slot = one_hot(iota((rows, rows), 0) == slot_rows)
    pick_tokens = lax.dot_general(reorder, row_of_slot, NT, preferred_element_type=F32).astype(BF16)
    ordered = dot(pick_tokens, tokens[...])
    gained[...] = (ordered * gain[...].astype(F32)).astype(BF16)
    squares = jnp.sum(ordered * ordered, axis=1, keepdims=True)
    side[:, 2 * KVCOLS:] = jnp.broadcast_to(squares, (rows, HEAD))

    wide_rows = parts * rows
    j = iota((rows, wide_rows), 1)
    slot_j = reversed_bits(j // block, stages) * local + j % local
    spread = one_hot(slot_j == iota((rows, wide_rows), 0))
    rows_bf = jnp.broadcast_to(slot_rows, (8, rows)).astype(F32).astype(BF16)
    row_j = dot(rows_bf, spread)[:1].astype(jnp.int32)
    out_row = iota((wide_rows, 1), 0)
    part_j = (iota((1, wide_rows), 1) % block) // local
    picks[...] = one_hot(jnp.logical_and(out_row % rows == row_j, out_row // rows == part_j))

    slot_id = iota((local, HEAD), 0)
    position = jnp.zeros((local, HEAD), F32)
    for l in range(local):
        position = jnp.where(slot_id == l, lengths[l].astype(F32), position)
    angle = position * freq[...]
    cosine = jnp.cos(angle)
    sine = jnp.where(iota((local, HEAD), 1) < HEAD // 2, -1.0, 1.0) * jnp.sin(angle)

    heads_rows = GROUP * local
    a = iota((heads_rows, heads_rows), 0)
    c = iota((heads_rows, heads_rows), 1)
    to_slots = one_hot((a % GROUP) * local + a // GROUP == c)
    head_a = ((a % block) // local) * per + a // block
    to_block = one_hot((a % local) * GROUP + head_a == c)

    def rs_copy(chunk, s):
        half = rows >> (s + 1)
        if s < stages - 1:
            start = (base[s] + (1 - bits[s]) * (n >> (s + 1))) * local
            src = (side if chunk == 0 else queries.at[chunk - 1]).at[pl.ds(pl.multiple_of(start, half), half)]
        else:
            src = side_out if chunk == 0 else query_out.at[chunk - 1]
        dst = side_in[s] if chunk == 0 else query_in[s].at[chunk - 1]
        return pltpu.make_async_remote_copy(
            src_ref=src, dst_ref=dst, send_sem=rs_send.at[chunk, s], recv_sem=rs_recv.at[chunk, s],
            device_id={"wide": partner[s]}, device_id_type=pl.DeviceIdType.MESH)

    def project(chunk):
        arrived(chunk)
        x = gained[...]
        if chunk == 0:
            side[:, :KVCOLS] = dot(x, wk[...])
            side[:, KVCOLS:2 * KVCOLS] = dot(x, wv[...])
        else:
            g = chunk - 1

            @pl.loop(0, QCOLS // 512)
            def _(i):
                at = pl.ds(pl.multiple_of(i * 512, 512), 512)
                queries[g, :, at] = dot(gained[...], wq[g, :, at])
        rs_copy(chunk, 0).start()

    def kept(chunk, s):
        half = rows >> (s + 1)
        buf = side if chunk == 0 else queries.at[chunk - 1]
        at = pl.ds(pl.multiple_of(base[s + 1] * local, half), half)
        return buf, at

    def reduce(chunk, s):
        rs_copy(chunk, s).wait()
        got = side_in[s] if chunk == 0 else query_in[s].at[chunk - 1]
        if s < stages - 2:
            buf, at = kept(chunk, s)
            buf[at, :] = buf[at, :] + got[...]
            rs_copy(chunk, s + 1).start()
            return None
        if s == stages - 2:
            buf, at = kept(chunk, s)
            value = buf[at, :] + got[...]
            low, high = value[:local], value[local:]
            first = bits[stages - 1] == 0
            (side_out if chunk == 0 else query_out.at[chunk - 1])[...] = jnp.where(first, high, low)
            rs_copy(chunk, s + 1).start()
            return jnp.where(first, low, high)
        return got[...]

    def rotate(value, cos, sin):
        return value * cos + pltpu.roll(value, HEAD // 2, 1) * sin

    def finish_side(value):
        scale = lax.rsqrt(value[:, 2 * KVCOLS:] / (width * n) + 1e-5)
        cos = cosine * scale
        sin = sine * scale
        for h in range(GROUP):
            cos_tile[pl.ds(h * local, local), :] = cos
            sin_tile[pl.ds(h * local, local), :] = sin
        for h in range(KV_HEADS):
            at = slice(h * HEAD, (h + 1) * HEAD)
            key = rotate(value[:, at], cos, sin).astype(BF16)
            new = (value[:, KVCOLS + h * HEAD:KVCOLS + (h + 1) * HEAD] * scale).astype(BF16)
            entries[0, :, at] = key
            entries[1, :, at] = new
            fresh[0, :, at] = key.astype(F32)
            fresh[1, :, at] = new.astype(F32)

    def attend(g, value):
        for h in range(GROUP):
            qs[pl.ds(h * local, local), :] = value[:, h * HEAD:(h + 1) * HEAD]
        query = rotate(qs[...], cos_tile[...], sin_tile[...]).astype(BF16)
        query = dot(to_slots, query).astype(BF16)
        at = slice(g * HEAD, (g + 1) * HEAD)
        factor = HEAD ** -0.5
        for l in range(local):
            q = query[l * GROUP:(l + 1) * GROUP]
            scores = lax.dot_general(q, kc[l, :, at], NT, preferred_element_type=F32) * factor
            scores = jnp.where(iota((GROUP, room), 1) < lengths[l], scores, -1e30)
            own = jnp.sum(q.astype(F32) * fresh[0, l:l + 1, at], axis=1, keepdims=True) * factor
            top = jnp.maximum(jnp.max(scores, axis=1, keepdims=True), own)
            weights = jnp.exp(scores - top)
            own_weight = jnp.exp(own - top)
            total = jnp.sum(weights, axis=1, keepdims=True) + own_weight
            mix = dot(weights.astype(BF16), vc[l, :, at])
            mix = mix + own_weight.astype(BF16).astype(F32) * fresh[1, l:l + 1, at]
            hs[pl.ds(l * GROUP, GROUP), :] = (mix / total).astype(BF16)
        mine = dot(to_block, hs[...]).astype(BF16)
        at_rows = pl.ds(pl.multiple_of(base[stages] * block, block), block)
        for p in range(per):
            gathered[g, at_rows, p * HEAD:(p + 1) * HEAD] = mine[p * block:(p + 1) * block]
        ag_copy(g, 0).start()

    def ag_copy(g, u):
        s = stages - 1 - u
        size = block << u
        at = pl.ds(pl.multiple_of(base[s + 1] * block, size), size)
        ref = gathered.at[g, at]
        return pltpu.make_async_remote_copy(
            src_ref=ref, dst_ref=ref, send_sem=ag_send.at[g, u], recv_sem=ag_recv.at[g, u],
            device_id={"wide": partner[s]}, device_id_type=pl.DeviceIdType.MESH)

    def emit(g):
        arrived(KV_HEADS + 2 + g)
        heads = dot(picks[...], gathered[g]).astype(BF16)
        part_cols = QCOLS // parts
        acc = total_out[...] if g else tokens[...].astype(F32)
        for p in range(parts):
            acc = acc + dot(heads[p * rows:(p + 1) * rows],
                            wo[pl.ds(g * QCOLS + p * part_cols, part_cols), :])
        if g < KV_HEADS - 1:
            total_out[...] = acc
        else:
            mixed[...] = acc.astype(BF16)

    pl.semaphore_wait(barrier, stages)
    chunks = KV_HEADS + 1
    held = {}
    for t in range(chunks + 2 * stages):
        if t < chunks:
            project(t)
            if t == 1:
                begin(chunks)
            if t >= 1:
                begin(chunks + t)
        for chunk in range(chunks):
            s = t - 1 - chunk
            if 0 <= s < stages:
                value = reduce(chunk, s)
                if s == stages - 2:
                    held[chunk] = value
                if s == stages - 1:
                    value = held.pop(chunk) + value
                    if chunk == 0:
                        finish_side(value)
                    else:
                        if chunk == 1:
                            arrived(chunks)
                        attend(chunk - 1, value)
            u = t - 1 - stages - chunk
            if chunk and 0 <= u < stages:
                ag_copy(chunk - 1, u).wait()
                if u < stages - 1:
                    ag_copy(chunk - 1, u + 1).start()
                else:
                    emit(chunk - 1)


def body(tokens, norm_gain, w_query, key_weight, value_weight, w_out,
         cache_keys, value_cache_slots, slot_fill_lengths, slot_rows, *, n):
    rows, width = tokens.shape
    local, room, _ = cache_keys.shape
    stages = n.bit_length() - 1
    out_width = w_out.shape[1]
    half = HEAD // 2
    freq = np.float32(500000.0) ** (-(np.float32(2.0) / np.float32(HEAD)) * np.arange(half, dtype=np.float32))
    freq = jnp.asarray(np.concatenate([freq, freq])[None, :].astype(np.float32))
    vmem = pl.BlockSpec(memory_space=pltpu.VMEM)
    anywhere = pl.BlockSpec(memory_space=pl.ANY)
    halves = [rows >> (s + 1) for s in range(stages)]
    chunks = KV_HEADS + 1
    wide_rows = 16 // local * rows
    scratch = [
        pltpu.VMEM((KV_HEADS, width, QCOLS), BF16),
        pltpu.VMEM((width, KVCOLS), BF16),
        pltpu.VMEM((width, KVCOLS), BF16),
        pltpu.VMEM(w_out.shape, BF16),
        pltpu.VMEM(cache_keys.shape, BF16),
        pltpu.VMEM(cache_keys.shape, BF16),
        pltpu.VMEM((rows, width), BF16),
        pltpu.VMEM((rows, SIDE), F32),
        pltpu.VMEM((KV_HEADS, rows, QCOLS), F32),
        *[pltpu.VMEM((h, SIDE), F32) for h in halves],
        *[pltpu.VMEM((KV_HEADS, h, QCOLS), F32) for h in halves],
        pltpu.VMEM((local, SIDE), F32),
        pltpu.VMEM((KV_HEADS, local, QCOLS), F32),
        pltpu.VMEM((KV_HEADS, wide_rows, QCOLS * local // 16), BF16),
        pltpu.VMEM((GROUP * local, HEAD), F32),
        pltpu.VMEM((GROUP * local, HEAD), BF16),
        pltpu.VMEM((GROUP * local, HEAD), F32),
        pltpu.VMEM((GROUP * local, HEAD), F32),
        pltpu.VMEM((2, local, KVCOLS), F32),
        pltpu.VMEM((wide_rows, wide_rows), BF16),
        pltpu.VMEM((rows, out_width), F32),
        pltpu.SemaphoreType.DMA((8 + KV_HEADS,)),
        pltpu.SemaphoreType.DMA((chunks, stages)),
        pltpu.SemaphoreType.DMA((chunks, stages)),
        pltpu.SemaphoreType.DMA((KV_HEADS, stages)),
        pltpu.SemaphoreType.DMA((KV_HEADS, stages)),
    ]
    return pl.pallas_call(
        functools.partial(kernel, n, stages, local, room, width),
        out_shape=(jax.ShapeDtypeStruct((rows, out_width), BF16),
                   jax.ShapeDtypeStruct((2, local, KVCOLS), BF16)),
        in_specs=[pl.BlockSpec(memory_space=pltpu.SMEM)] + [vmem] * 4 + [anywhere] * 6,
        out_specs=(vmem, vmem),
        scratch_shapes=scratch,
        compiler_params=pltpu.CompilerParams(
            collective_id=0, has_side_effects=True, vmem_limit_bytes=60 * 1024 * 1024),
    )(slot_fill_lengths, tokens, norm_gain.reshape(1, width), slot_rows.reshape(1, rows), freq,
      w_query, key_weight, value_weight, w_out, cache_keys, value_cache_slots)


def solution(mesh):
    placed = (
        P("groups", "wide"),
        P("wide"),
        P("wide", None),
        P("wide", None),
        P("wide", None),
        P(None, "wide"),
        P(("groups", "wide"), None, None),
        P(("groups", "wide"), None, None),
        P(("groups", "wide")),
        P("groups"),
    )
    return jax.shard_map(
        functools.partial(body, n=mesh.shape["wide"]),
        mesh=mesh,
        in_specs=placed,
        out_specs=(P("groups", "wide"), P(None, ("groups", "wide"), None)),
        check_vma=False,
    )
```
